128 devices in a mesh: fsdp: 16 (over x, z), tp: 8 (over y, core).
Axes of the slice: x: 4, y: 4, z: 4, core: 2. Of those that a mesh axis runs over, the one named last changes fastest.
Arguments:
- old_master: float32 [256, 4300, 128], P(('fsdp', 'tp')), may hold values from -0.046875 to 0.046875
- old_momentum: float32 [256, 4300, 128], P(('fsdp', 'tp')), may hold values from -6 to 6
- old_variance: float32 [256, 4300, 128], P(('fsdp', 'tp')), may hold values from 0.1 to 2
- flat_offsets: int32 [257], replicated, may hold values from 0 to 917504, as said below
- hidden_acts: bfloat16 [2048, 14336], P('fsdp', 'tp'), may hold values from -6 to 6
- out_grad: bfloat16 [2048, 8192], P('tp', 'fsdp'), may hold values from -0.29882812 to 0.29882812
Outputs:
- output: bfloat16 [2048, 8192], P('tp', 'fsdp')
- new_master: float32 [14336, 8192], P('tp', 'fsdp')
- new_momentum: float32 [14336, 8192], P('tp', 'fsdp')
- new_variance: float32 [14336, 8192], P('tp', 'fsdp')
The draws below stay inside these ranges and needn't reach their ends.
Inputs may be any that keep to these rules, and one draw needn't show every extreme that they name: flat_offsets rises from 0 to 917504; entry k lies within 358 of k * 3584, and differs from it where k is a multiple of 32 strictly between 0 and 256; each piece holds between 2868 and 4300 granules, the largest reached by some piece in every draw; entries of a piece past its length are not part of the slab.
All inputs are finite; a program needn't handle non-finite values.
Results may differ from the reference program's by a relative error of at most 0.013.
Values may be sent and summed in bfloat16 or wider, within the bound.
No kernel may reach another device: no remote copies, remote signals or barrier semaphores. Data moves between devices by JAX's collectives and lax.ppermute only.
A program may use at most 192 MiB of HBM per device.

```python
import math
import jax
import jax.numpy as jnp
from jax import lax

D = 8192
FF = 14336
GRANULE = 128
STEP = 100
TOKENS = 2048
OLD_OWNERS = 256
MEAN_PIECE = 3584
JITTER = 358
CAPACITY = 550400
N_TP = 8


def draw_flat_offsets(key, part):
    key = jax.random.fold_in(key, 7)
    key_shift, key_pick, key_block, key_edge, key_sign = jax.random.split(key, 5)
    positions = jnp.arange(OLD_OWNERS + 1, dtype=jnp.int32)
    block_len = OLD_OWNERS // N_TP
    shifts = jax.random.randint(key_shift, (OLD_OWNERS + 1,), -JITTER, JITTER + 1, dtype=jnp.int32)
    edge_size = jax.random.randint(key_edge, (OLD_OWNERS + 1,), 1, JITTER + 1, dtype=jnp.int32)
    edge_sign = 2 * jax.random.randint(key_sign, (OLD_OWNERS + 1,), 0, 2, dtype=jnp.int32) - 1
    shifts = jnp.where(positions % block_len == 0, edge_sign * edge_size, shifts)
    shifts = jnp.where(positions == block_len, JITTER, shifts)
    shifts = jnp.where(positions == 2 * block_len, -JITTER, shifts)
    chosen = jax.random.randint(key_block, (), 0, N_TP, dtype=jnp.int32) * block_len + jax.random.randint(key_pick, (), 1, block_len - 1, dtype=jnp.int32)
    shifts = jnp.where(positions == chosen, -JITTER, shifts)
    shifts = jnp.where(positions == chosen + 1, JITTER, shifts)
    shifts = jnp.where((positions == 0) | (positions == OLD_OWNERS), 0, shifts)
    return positions * MEAN_PIECE + shifts


def steps_of(rng, extent, cuts, low, top_value):
    level = 1.0
    for dim, blocks in cuts:
        heights = jax.random.uniform(jax.random.fold_in(jax.random.fold_in(rng, 6), dim), (blocks,), jnp.float32, low / len(cuts), top_value / len(cuts))
        level = level * jnp.repeat(jnp.exp(heights), extent[dim] // blocks).reshape((-1,) + (1,) * (len(extent) - 1 - dim))
    return level


def gaussian(key, dims, scale, most, cuts=(), kind=jnp.bfloat16):
    drawn = jax.random.normal(key, dims, jnp.float32) * scale
    if len(cuts) > 0:
        drawn = steps_of(key, dims, cuts, -0.22, 0.18) * drawn
    return jnp.clip(drawn, min=-most, max=most).astype(kind)


def setup_inputs(seed: int = 0) -> dict:
    keys = jax.random.split(jax.random.key(seed), 7)
    old_master = gaussian(keys[0], (OLD_OWNERS, CAPACITY // GRANULE, GRANULE), FF ** -0.5, 0.046875, ((0, 128),), jnp.float32)
    old_momentum = gaussian(keys[1], (OLD_OWNERS, CAPACITY // GRANULE, GRANULE), 1.0, 6.0, ((0, 128),), jnp.float32)
    old_variance = jnp.clip(jnp.exp(math.log(2.0) - 2.9957323 * jax.random.uniform(keys[2], (OLD_OWNERS, CAPACITY // GRANULE, GRANULE), jnp.float32) ** steps_of(keys[2], (OLD_OWNERS, CAPACITY // GRANULE, GRANULE), ((0, 128),), -0.2, 0.2)), 0.1, 2.0)
    flat_offsets = draw_flat_offsets(jax.random.fold_in(keys[6], 71), 0)
    hidden_acts = gaussian(keys[4], (TOKENS, FF), 1.0, 6.0, ((0, 16), (1, 8)))
    out_grad = gaussian(keys[5], (TOKENS, D), 0.05, 0.29882812, ((0, 8), (1, 16)))
    return {"old_master": old_master, "old_momentum": old_momentum, "old_variance": old_variance, "flat_offsets": flat_offsets, "hidden_acts": hidden_acts, "out_grad": out_grad}


beta_first = 0.9
beta_second = 0.95
epsilon = 1e-08
decay_rate = 0.1
learn_rate = 0.001

def assemble(pieces, offsets):
    pieces = pieces.reshape(OLD_OWNERS, CAPACITY)
    buffer = jnp.zeros((FF * D + CAPACITY,), jnp.float32)
    positions = jnp.arange(CAPACITY)

    def place_piece(owner_idx, buffer):
        start_at = offsets[owner_idx] * GRANULE
        span_len = (offsets[owner_idx + 1] - offsets[owner_idx]) * GRANULE
        kept = jnp.where(positions < span_len, pieces[owner_idx], jnp.float32(0.0))
        return lax.dynamic_update_slice(buffer, kept, (start_at,))
    buffer = lax.fori_loop(0, OLD_OWNERS, place_piece, buffer)
    return buffer[:FF * D].reshape(FF, D)

def reference(old_master, old_momentum, old_variance, flat_offsets, hidden_acts, out_grad):
    master = assemble(old_master, flat_offsets)
    momentum = assemble(old_momentum, flat_offsets)
    variance = assemble(old_variance, flat_offsets)
    weight = master.astype(jnp.bfloat16)
    block_rows = FF // N_TP
    total = jnp.zeros((TOKENS, D), jnp.float32)
    for block_idx in range(N_TP):
        lower = block_idx * block_rows
        partial_value = jnp.dot(hidden_acts[:, lower:lower + block_rows], weight[lower:lower + block_rows], preferred_element_type=jnp.float32).astype(jnp.bfloat16)
        total = total + partial_value.astype(jnp.float32)
    output = total.astype(jnp.bfloat16)
    weight_grad = lax.dot_general(hidden_acts, out_grad, (((0,), (0,)), ((), ())), preferred_element_type=jnp.float32)
    new_momentum = beta_first * momentum + (1.0 - beta_first) * weight_grad
    new_variance = beta_second * variance + (1.0 - beta_second) * weight_grad * weight_grad
    fix_first = 1.0 - beta_first ** STEP
    fix_second = 1.0 - beta_second ** STEP
    update = new_momentum / fix_first / (jnp.sqrt(new_variance / fix_second) + epsilon) + decay_rate * master
    new_master = master - learn_rate * update
    return (output, new_master, new_momentum, new_variance)
```

```python
import functools

import jax
import jax.numpy as jnp
from jax import lax
from jax.experimental import pallas as pl
from jax.experimental.pallas import tpu as pltpu
from jax.sharding import PartitionSpec as P

LANES = 128
STEP = 100
AXES = ("fsdp", "tp")
N_FSDP, N_TP = 16, 8
N_ALL = N_FSDP * N_TP
ROW_GRANULES = 64
ROWS = 112
OWN = ROWS * ROW_GRANULES
COLS = 512
ROUNDS = 16
EDGE = 384
GRAN = 4300
TABLE = 2 * GRAN
FRONT = 1792
BACK = 1080

beta_first = 0.9
beta_second = 0.95
epsilon = 1e-08
decay_rate = 0.1
learn_rate = 0.001

PHASES = ((0,), (1, 2))


def source_of(f, t):
    return f * N_TP + t


def target_column(round_id, f, t):
    rx, rz = divmod(round_id, 4)
    x, z, y, c = f // 4, f % 4, t // 2, t % 2
    return ((x + rx + 4 - y + 2 * c) % 4) * 4 + (z + 2 * c + rz) % 4


def sender_block(round_id, f, t):
    rx, rz = divmod(round_id, 4)
    xp, zp, yp, cp = f // 4, f % 4, t // 2, t % 2
    w = (zp + 8 - 2 * cp - rz) % 4
    b, c = w % 2, w // 2
    y = (yp + rx + 2 * c + 4 - xp) % 4
    return b * N_TP + y * 2 + c


def round_pairs(round_id):
    pairs = []
    for f in range(N_FSDP):
        for t in range(N_TP):
            pairs.append((source_of(f, t), source_of(target_column(round_id, f, t), f // 2)))
    return pairs


def edge_kernel(flat, *refs):
    tables, (to_left, to_right) = refs[:3], refs[3:5]
    heads, tails, sems = refs[5:]
    copies = []
    for k in range(3):
        head = pltpu.make_async_copy(
            tables[k].at[pl.ds(0, 768)], heads.at[k, pl.ds(1536, 768)], sems.at[k, 0]
        )
        tail = pltpu.make_async_copy(
            tables[k].at[pl.ds(6448, 2152)], tails.at[k, pl.ds(0, 2152)], sems.at[k, 1]
        )
        head.start()
        tail.start()
        copies.append((head, tail))
    s = source_of(lax.axis_index("fsdp"), lax.axis_index("tp"))
    nominal = s * OWN
    first, middle, last = flat[2 * s], flat[2 * s + 1], flat[2 * s + 2]
    ids = lax.broadcasted_iota(jnp.int32, (EDGE, LANES), 0)
    left_at = nominal - EDGE - first
    right_at = nominal + OWN - middle
    left_ok = ids + left_at >= 0
    right_ok = ids + right_at < last - middle
    for k in range(3):
        copies[k][0].wait()
        copies[k][1].wait()
        left = heads[k, pl.ds(1536 + 2 * left_at, EDGE, stride=2), :]
        right = tails[k, pl.ds(2 * right_at + 1 - 6448, EDGE, stride=2), :]
        to_left[k * EDGE : (k + 1) * EDGE, :] = jnp.where(left_ok, left, 0.0).astype(jnp.bfloat16)
        to_right[k * EDGE : (k + 1) * EDGE, :] = jnp.where(right_ok, right, 0.0).astype(
            jnp.bfloat16
        )


def pack_kernel(which, flat, *refs):
    count = len(which)
    tables = refs[:count]
    from_left, from_right = refs[count : count + 2]
    outs = refs[count + 2 : count + 2 + ROUNDS]
    held, left_edge, right_edge, sems = refs[count + 2 + ROUNDS :]
    copies = []
    for k in range(count):
        copy = pltpu.make_async_copy(
            tables[k], held.at[k, pl.ds(FRONT, TABLE)], sems.at[k]
        )
        copy.start()
        copies.append(copy)
    f, t = lax.axis_index("fsdp"), lax.axis_index("tp")
    s = source_of(f, t)
    nominal = s * OWN
    low = flat[2 * s] - nominal
    cut = flat[2 * s + 1] - nominal
    high = flat[2 * s + 2] - nominal
    for k in range(count):
        at = which[k] * EDGE
        left_edge[k, 0:EDGE, :] = from_left[at : at + EDGE, :].astype(jnp.float32)
        right_edge[k, 1024 - EDGE : 1024, :] = from_right[at : at + EDGE, :].astype(jnp.float32)
    ids = lax.broadcasted_iota(jnp.int32, (16, LANES), 0) * ROW_GRANULES
    stride = 2 * ROW_GRANULES
    for k in range(count):
        copies[k].wait()
        for r in range(ROUNDS):
            column = target_column(r, f, t) * 4
            for q in range(4):
                c = column + q
                at_a = FRONT + 2 * (c - low)
                at_b = FRONT + 2 * (c - cut) + 1

                def rows_of(at, row, n):
                    return held[k, pl.ds(at + row * stride, n, stride=stride), :]

                def put(row, n, value):
                    outs[r][k * ROWS + row : k * ROWS + row + n, q * LANES : (q + 1) * LANES] = (
                        value.astype(jnp.bfloat16)
                    )

                edge = left_edge[k, pl.ds(c, 16, stride=ROW_GRANULES), :]
                put(0, 16, jnp.where(ids + c < low, edge, rows_of(at_a, 0, 16)))
                put(16, 32, rows_of(at_a, 16, 32))
                put(
                    48,
                    16,
                    jnp.where(
                        ids + c + 48 * ROW_GRANULES < cut,
                        rows_of(at_a, 48, 16),
                        rows_of(at_b, 48, 16),
                    ),
                )
                put(64, 32, rows_of(at_b, 64, 32))
                edge = right_edge[k, pl.ds(c, 16, stride=ROW_GRANULES), :]
                put(
                    96,
                    16,
                    jnp.where(ids + c + 96 * ROW_GRANULES >= high, edge, rows_of(at_b, 96, 16)),
                )


def product_kernel(acts, *refs):
    parts, out, weight = refs[:ROUNDS], refs[ROUNDS], refs[ROUNDS + 1]

    @pl.when(pl.program_id(0) == 0)
    def _():
        f, t = lax.axis_index("fsdp"), lax.axis_index("tp")
        for r in range(ROUNDS):
            at = pl.multiple_of(sender_block(r, f, t) * ROWS, 16)
            weight[pl.ds(at, ROWS), :] = parts[r][...]

    out[...] = jnp.dot(acts[...], weight[...], preferred_element_type=jnp.float32).astype(
        jnp.bfloat16
    )


def update_kernel(where, *refs):
    n_phase = 1 + max(phase for phase, _ in where)
    arrived = [refs[p * ROUNDS : (p + 1) * ROUNDS] for p in range(n_phase)]
    at = n_phase * ROUNDS
    grad = refs[at]
    new_master, new_momentum, new_variance = refs[at + 1 : at + 4]
    held, grads, results, in_sems, out_sems = refs[at + 4 :]
    f, t = lax.axis_index("fsdp"), lax.axis_index("tp")
    rows = [pl.multiple_of(sender_block(r, f, t) * ROWS, 16) for r in range(ROUNDS)]
    copies = []
    for r in range(ROUNDS):
        mine = []
        for k in range(3):
            phase, row = where[k]
            mine.append(
                pltpu.make_async_copy(
                    arrived[phase][r].at[pl.ds(row, ROWS)], held.at[r, k], in_sems.at[r, k]
                )
            )
        mine.append(
            pltpu.make_async_copy(grad.at[pl.ds(rows[r], ROWS)], grads.at[r], in_sems.at[r, 3])
        )
        for copy in mine:
            copy.start()
        copies.append(mine)
    fix_first = 1.0 - beta_first**STEP
    fix_second = 1.0 - beta_second**STEP
    leaving = []
    for r in range(ROUNDS):
        for copy in copies[r]:
            copy.wait()
        master = held[r, 0].astype(jnp.float32)
        momentum = held[r, 1].astype(jnp.float32)
        variance = held[r, 2].astype(jnp.float32)
        g = grads[r]
        m = beta_first * momentum + (1.0 - beta_first) * g
        v = beta_second * variance + (1.0 - beta_second) * g * g
        update = m / fix_first / (jnp.sqrt(v / fix_second) + epsilon) + decay_rate * master
        results[r, 0] = master - learn_rate * update
        results[r, 1] = m
        results[r, 2] = v
        for k, out in enumerate((new_master, new_momentum, new_variance)):
            copy = pltpu.make_async_copy(
                results.at[r, k], out.at[pl.ds(rows[r], ROWS)], out_sems.at[r, k]
            )
            copy.start()
            leaving.append(copy)
    for copy in leaving:
        copy.wait()


def any_spec():
    return pl.BlockSpec(memory_space=pl.ANY)


def smem_spec():
    return pl.BlockSpec(memory_space=pltpu.SMEM)


def vmem_spec():
    return pl.BlockSpec(memory_space=pltpu.VMEM)


def make_edges(flat, tables):
    shape = jax.ShapeDtypeStruct((3 * EDGE, LANES), jnp.bfloat16)
    return pl.pallas_call(
        edge_kernel,
        out_shape=(shape, shape),
        in_specs=[smem_spec()] + [any_spec()] * 3,
        out_specs=(vmem_spec(), vmem_spec()),
        scratch_shapes=[
            pltpu.VMEM((3, 2304, LANES), jnp.float32),
            pltpu.VMEM((3, 2240, LANES), jnp.float32),
            pltpu.SemaphoreType.DMA((3, 2)),
        ],
        compiler_params=pltpu.CompilerParams(vmem_limit_bytes=24 * 2**20),
        cost_estimate=pl.CostEstimate(flops=0, bytes_accessed=6 * 2**20, transcendentals=0),
        name="edges",
    )(flat, *tables)


def make_messages(which, flat, tables, from_left, from_right):
    count = len(which)
    shape = jax.ShapeDtypeStruct((count * ROWS, COLS), jnp.bfloat16)
    return pl.pallas_call(
        functools.partial(pack_kernel, which),
        out_shape=(shape,) * ROUNDS,
        in_specs=[smem_spec()] + [any_spec()] * count + [vmem_spec()] * 2,
        out_specs=(vmem_spec(),) * ROUNDS,
        scratch_shapes=[
            pltpu.VMEM((count, FRONT + TABLE + BACK, LANES), jnp.float32),
            pltpu.VMEM((count, 1024, LANES), jnp.float32),
            pltpu.VMEM((count, 1024, LANES), jnp.float32),
            pltpu.SemaphoreType.DMA((count,)),
        ],
        compiler_params=pltpu.CompilerParams(vmem_limit_bytes=40 * 2**20),
        cost_estimate=pl.CostEstimate(
            flops=0, bytes_accessed=count * 7 * 2**20, transcendentals=0
        ),
        name="pack",
    )(flat, *[tables[k] for k in which], from_left, from_right)


def make_product(acts, parts):
    tokens, depth = acts.shape
    tile = 256
    return pl.pallas_call(
        product_kernel,
        out_shape=jax.ShapeDtypeStruct((tokens, COLS), jnp.bfloat16),
        grid=(tokens // tile,),
        in_specs=[pl.BlockSpec((tile, depth), lambda i: (i, 0))]
        + [pl.BlockSpec((ROWS, COLS), lambda i: (0, 0))] * ROUNDS,
        out_specs=pl.BlockSpec((tile, COLS), lambda i: (i, 0)),
        scratch_shapes=[pltpu.VMEM((depth, COLS), jnp.bfloat16)],
        compiler_params=pltpu.CompilerParams(vmem_limit_bytes=24 * 2**20),
        cost_estimate=pl.CostEstimate(
            flops=2 * tokens * depth * COLS, bytes_accessed=12 * 2**20, transcendentals=0
        ),
        name="product",
    )(acts, *parts)


def make_update(arrived, where, grad):
    shape = jax.ShapeDtypeStruct(grad.shape, jnp.float32)
    return pl.pallas_call(
        functools.partial(update_kernel, where),
        out_shape=(shape,) * 3,
        in_specs=[any_spec()] * (len(arrived) * ROUNDS + 1),
        out_specs=(any_spec(),) * 3,
        scratch_shapes=[
            pltpu.VMEM((ROUNDS, 3, ROWS, COLS), jnp.bfloat16),
            pltpu.VMEM((ROUNDS, ROWS, COLS), jnp.float32),
            pltpu.VMEM((ROUNDS, 3, ROWS, COLS), jnp.float32),
            pltpu.SemaphoreType.DMA((ROUNDS, 4)),
            pltpu.SemaphoreType.DMA((ROUNDS, 3)),
        ],
        compiler_params=pltpu.CompilerParams(vmem_limit_bytes=32 * 2**20),
        cost_estimate=pl.CostEstimate(
            flops=30 * grad.size, bytes_accessed=20 * 2**20, transcendentals=0
        ),
        name="update",
    )(*[a for phase in arrived for a in phase], grad)


def on_device(old_master, old_momentum, old_variance, flat_offsets, hidden_acts, out_grad):
    acts = lax.all_gather(hidden_acts, "fsdp", axis=0, tiled=True)
    tables = [
        jnp.transpose(old, (1, 0, 2)).reshape(TABLE, LANES)
        for old in (old_master, old_momentum, old_variance)
    ]
    to_left, to_right = make_edges(flat_offsets, tables)
    from_left = lax.ppermute(to_right, AXES, [(s, (s + 1) % N_ALL) for s in range(N_ALL)])
    from_right = lax.ppermute(to_left, AXES, [(s, (s - 1) % N_ALL) for s in range(N_ALL)])
    arrived = []
    where = [None] * 3
    for number, which in enumerate(PHASES):
        messages = make_messages(which, flat_offsets, tables, from_left, from_right)
        arrived.append(
            [lax.ppermute(messages[r], AXES, round_pairs(r)) for r in range(ROUNDS)]
        )
        for k, tensor in enumerate(which):
            where[tensor] = (number, k * ROWS)
    grads_out = lax.all_gather(out_grad, "tp", axis=0, tiled=True)
    product = make_product(acts, arrived[0])
    output = lax.psum_scatter(product, "tp", scatter_dimension=0, tiled=True)
    weight_grad = lax.dot_general(
        acts, grads_out, (((0,), (0,)), ((), ())), preferred_element_type=jnp.float32
    )
    new_master, new_momentum, new_variance = make_update(arrived, where, weight_grad)
    return (output, new_master, new_momentum, new_variance)


def solution(mesh):
    return jax.shard_map(
        on_device,
        mesh=mesh,
        in_specs=(
            P(("fsdp", "tp"), None, None),
            P(("fsdp", "tp"), None, None),
            P(("fsdp", "tp"), None, None),
            P(),
            P("fsdp", "tp"),
            P("tp", "fsdp"),
        ),
        out_specs=(P("tp", "fsdp"), P("tp", "fsdp"), P("tp", "fsdp"), P("tp", "fsdp")),
        check_vma=False,
    )
```

```python
import functools

import jax
import jax.numpy as jnp
from jax import lax
from jax.experimental import pallas as pl
from jax.experimental.pallas import tpu as pltpu
from jax.sharding import PartitionSpec as P

LANES = 128
STEP = 100
AXES = ("fsdp", "tp")
N_FSDP, N_TP = 16, 8
N_ALL = N_FSDP * N_TP
ROW_GRANULES = 64
ROWS = 112
PAIR = 2 * ROWS
SPAN = 128
OWN = ROWS * ROW_GRANULES
COLS = 512
ROUNDS = 8
CHUNK = 16
EDGE = 384
GRAN = 4300
TABLE = 2 * GRAN
FRONT = 2816
BACK = 1400
VMEM_LIMIT = 60 * 2**20

beta_first = 0.9
beta_second = 0.95
epsilon = 1e-08
decay_rate = 0.1
learn_rate = 0.001

WAIT_FOR = 1
PHASES = ((0,), (1, 2))


def source_of(f, t):
    return f * N_TP + t


def target_column(round_id, f, t):
    rv, ru = divmod(round_id, 4)
    x, z, y, c = f // 4, f % 4, t // 2, t % 2
    return ((x + 4 - y + ru + 2 * c) % 4) * 4 + (z + rv + 2 * c) % 4


def sender_block(round_id, f, t):
    rv, ru = divmod(round_id, 4)
    xp, zp, yp, cp = f // 4, f % 4, t // 2, t % 2
    w = (zp + 8 - 2 * cp - rv) % 4
    b, c = w % 2, w // 2
    y = (yp + ru + 2 * c + 4 - xp) % 4
    return b * 4 + y


def all_pairs(target):
    return [
        (source_of(f, t), source_of(*target(f, t))) for f in range(N_FSDP) for t in range(N_TP)
    ]


def round_pairs(round_id):
    return all_pairs(lambda f, t: (target_column(round_id, f, t), f // 2))


def sibling_pairs():
    return all_pairs(lambda f, t: (f, t ^ 1))


def edge_pairs(same_core):
    pairs = []
    for s in range(N_ALL):
        pair, core = s // 2, s % 2
        pair = (pair + (1 if core else -1)) % (N_ALL // 2)
        pairs.append((s, pair * 2 + (core if same_core else 1 - core)))
    return pairs


def along_y(shift):
    return all_pairs(lambda f, t: (f, (t + 2 * shift) % N_TP))


def on_core(body):
    core = lax.axis_index("tp") % 2
    for static in range(2):
        pl.when(core == static)(functools.partial(body, static))


def load_tables(tables, held, sems):
    copies = []
    for k, table in enumerate(tables):
        copy = pltpu.make_async_copy(table, held.at[k, pl.ds(FRONT, TABLE)], sems.at[k])
        copy.start()
        copies.append(copy)
    return copies


def own_rows(held, flat, k, core, row, column):
    s = source_of(lax.axis_index("fsdp"), lax.axis_index("tp"))
    base = (s // 2) * (PAIR * ROW_GRANULES)
    at = (ROWS * core + row) * ROW_GRANULES + column
    stride = 2 * ROW_GRANULES
    cut = flat[2 * s + 1] - base

    def first():
        return held[k, pl.ds(FRONT + 2 * (at + base - flat[2 * s]), 16, stride=stride), :]

    def second():
        return held[k, pl.ds(FRONT + 2 * (at - cut) + 1, 16, stride=stride), :]

    if row < 48:
        return first()
    if row > 48:
        return second()
    ids = lax.broadcasted_iota(jnp.int32, (16, LANES), 0) * ROW_GRANULES
    return jnp.where(ids + at < cut, first(), second())


def swap_kernel(count, flat, *refs):
    tables = refs[:count]
    out, edge, held, sems = refs[count:]
    copies = load_tables(tables, held, sems)
    f, t = lax.axis_index("fsdp"), lax.axis_index("tp")
    s = source_of(f, t)
    left_at = s * OWN - EDGE - flat[2 * s]
    right_at = s * OWN + OWN - flat[2 * s + 1]

    def put(core):
        for k in range(count):
            copies[k].wait()
            at = FRONT + (2 * right_at + 1 if core else 2 * left_at)
            edge[k * EDGE : (k + 1) * EDGE, :] = held[k, pl.ds(at, EDGE, stride=2), :].astype(
                jnp.bfloat16
            )
            for r in range(ROUNDS):
                for q in range(4):
                    column = target_column(r, f, t + 1 - 2 * core) * 4 + q
                    for j in range(SPAN // 16):
                        at = (k * ROUNDS + r) * SPAN + j * 16
                        out[at : at + 16, q * LANES : (q + 1) * LANES] = own_rows(
                            held, flat, k, core, 16 * (j - core), column
                        ).astype(jnp.bfloat16)

    on_core(put)


def pack_kernel(flat, *refs):
    count = 3
    tables = refs[:count]
    theirs, same, other = refs[count : count + 3]
    refs = refs[count + 3 :]
    outs = [refs[n * ROUNDS : (n + 1) * ROUNDS] for n in range(len(PHASES))]
    held, left_edge, right_edge, sems = refs[len(PHASES) * ROUNDS :]
    copies = load_tables(tables, held, sems)
    f, t = lax.axis_index("fsdp"), lax.axis_index("tp")
    s = source_of(f, t)
    base = (s // 2) * (PAIR * ROW_GRANULES)
    low = flat[2 * s - 2 * (t % 2)] - base
    middle = flat[2 * s - 2 * (t % 2) + 2] - base
    high = flat[2 * s - 2 * (t % 2) + 4] - base
    ids = lax.broadcasted_iota(jnp.int32, (16, LANES), 0) * ROW_GRANULES

    def put(core):
        if core == 0:
            from_left, from_right = other, same
        else:
            from_left, from_right = same, other
        for k in range(count):
            at = k * EDGE
            left_edge[k, 0:EDGE, :] = from_left[at : at + EDGE, :].astype(jnp.float32)
            right_edge[k, 1024 - EDGE : 1024, :] = from_right[at : at + EDGE, :].astype(
                jnp.float32
            )
        for k in range(count):
            copies[k].wait()
            phase = [n for n, which in enumerate(PHASES) if k in which][0]
            first_row = PHASES[phase].index(k) * PAIR
            for r in range(ROUNDS):
                out = outs[phase][r]
                for w in range(PAIR // 16):
                    mine = w <= 7 if core == 0 else w >= 6
                    his = w >= 6 if core == 0 else w <= 7
                    j = w - 6 if core == 0 else w
                    at = (k * ROUNDS + r) * SPAN + j * 16
                    row = first_row + w * 16
                    if his and not mine and 0 < w < 13:
                        out[row : row + 16, :] = theirs[at : at + 16, :]
                        continue
                    for q in range(4):
                        column = target_column(r, f, t) * 4 + q
                        lanes = slice(q * LANES, (q + 1) * LANES)
                        place = ids + w * 16 * ROW_GRANULES + column
                        if mine:
                            value = own_rows(held, flat, k, core, 16 * w - ROWS * core, column)
                        if his:
                            other_value = theirs[at : at + 16, lanes].astype(jnp.float32)
                            if mine:
                                own = place < middle if core == 0 else place >= middle
                                value = jnp.where(own, value, other_value)
                            else:
                                value = other_value
                        if w == 0:
                            edge = left_edge[k, pl.ds(column, 16, stride=ROW_GRANULES), :]
                            value = jnp.where(place < low, edge, value)
                        if w == 13:
                            edge = right_edge[k, pl.ds(column, 16, stride=ROW_GRANULES), :]
                            value = jnp.where(place >= high, edge, value)
                        out[row : row + 16, lanes] = value.astype(jnp.bfloat16)

    on_core(put)


def assemble(parts, weight):
    f, t = lax.axis_index("fsdp"), lax.axis_index("tp")
    for r in range(ROUNDS):
        at = pl.multiple_of(sender_block(r, f, t) * PAIR, 32)
        weight[pl.ds(at, PAIR), :] = parts[r][...]


def product_kernel(core, acts, *refs):
    parts, out, weight = refs[:ROUNDS], refs[ROUNDS], refs[ROUNDS + 1]
    pl.when(pl.program_id(0) == 0)(functools.partial(assemble, parts, weight))
    out[...] = jnp.dot(acts[...], weight[...], preferred_element_type=jnp.float32).astype(
        jnp.bfloat16
    )


def pair_kernel(mine, theirs, *outs):
    y = lax.axis_index("tp") // 2
    rows = mine.shape[0] // 4
    for d in range(4):
        at = pl.multiple_of(((y + d) % 4) * rows, 32)
        total = mine[pl.ds(at, rows), :].astype(jnp.float32) + theirs[pl.ds(at, rows), :].astype(
            jnp.float32
        )
        outs[d][...] = total.astype(jnp.bfloat16)


def update_kernel(where, rounds, resumed, *refs):
    n_phase = 1 + max(phase for phase, _ in where)
    count = len(rounds)
    arrived = [refs[p * count : (p + 1) * count] for p in range(n_phase)]
    at = n_phase * count
    grad = refs[at]
    at += 3 if resumed else 0
    new_master, new_momentum, new_variance = refs[at + 1 : at + 4]
    held, grads, results, in_sems, out_sems = refs[at + 4 :]
    f, t = lax.axis_index("fsdp"), lax.axis_index("tp")
    rows = [pl.multiple_of(sender_block(r, f, t) * PAIR, 32) for r in rounds]
    copies = []
    for r in range(count):
        mine = []
        for k in range(3):
            phase, row = where[k]
            mine.append(
                pltpu.make_async_copy(
                    arrived[phase][r].at[pl.ds(row, PAIR)], held.at[r, k], in_sems.at[r, k]
                )
            )
        mine.append(
            pltpu.make_async_copy(grad.at[pl.ds(rows[r], PAIR)], grads.at[r], in_sems.at[r, 3])
        )
        for copy in mine:
            copy.start()
        copies.append(mine)
    scale_first = 1.0 / (1.0 - beta_first**STEP)
    scale_second = 1.0 / (1.0 - beta_second**STEP)
    leaving = []
    for r in range(count):
        for copy in copies[r]:
            copy.wait()

        @pl.loop(0, PAIR // CHUNK, unroll=2)
        def _(step, r=r):
            chunk = pl.ds(pl.multiple_of(step * CHUNK, CHUNK), CHUNK)
            master = held[r, 0, chunk, :].astype(jnp.float32)
            momentum = held[r, 1, chunk, :].astype(jnp.float32)
            variance = held[r, 2, chunk, :].astype(jnp.float32)
            g = grads[r, chunk, :]
            m = beta_first * momentum + (1.0 - beta_first) * g
            v = beta_second * variance + (1.0 - beta_second) * g * g
            scaled = v * scale_second
            below = scaled * lax.rsqrt(scaled) + epsilon
            guess = pl.reciprocal(below, approx=True)
            inverse = guess * (2.0 - below * guess)
            change = (learn_rate * scale_first) * m * inverse
            results[r, 0, chunk, :] = (1.0 - learn_rate * decay_rate) * master - change
            results[r, 1, chunk, :] = m
            results[r, 2, chunk, :] = v

        for k, out in enumerate((new_master, new_momentum, new_variance)):
            copy = pltpu.make_async_copy(
                results.at[r, k], out.at[pl.ds(rows[r], PAIR)], out_sems.at[r, k]
            )
            copy.start()
            leaving.append(copy)
    for copy in leaving:
        copy.wait()


def any_spec():
    return pl.BlockSpec(memory_space=pl.ANY)


def hbm_spec():
    return pl.BlockSpec(memory_space=pltpu.HBM)


def smem_spec():
    return pl.BlockSpec(memory_space=pltpu.SMEM)


def vmem_spec():
    return pl.BlockSpec(memory_space=pltpu.VMEM)


def table_scratch(count):
    return [
        pltpu.VMEM((count, FRONT + TABLE + BACK, LANES), jnp.float32),
        pltpu.SemaphoreType.DMA((count,)),
    ]


def lasting(microseconds):
    return pl.CostEstimate(
        flops=0, bytes_accessed=int(microseconds * 3.3e6), transcendentals=0
    )


def make_swap(flat, tables):
    count = len(tables)
    return pl.pallas_call(
        functools.partial(swap_kernel, count),
        out_shape=(
            jax.ShapeDtypeStruct((count * ROUNDS * SPAN, COLS), jnp.bfloat16),
            jax.ShapeDtypeStruct((count * EDGE, LANES), jnp.bfloat16),
        ),
        in_specs=[smem_spec()] + [hbm_spec()] * count,
        out_specs=(vmem_spec(),) * 2,
        scratch_shapes=table_scratch(count),
        compiler_params=pltpu.CompilerParams(vmem_limit_bytes=VMEM_LIMIT),
        cost_estimate=lasting(1 + 3 * count),
        name="swap",
    )(flat, *tables)


def collect_kernel(own, *refs):
    parts, out = (own, *refs[:3]), refs[3]
    y = lax.axis_index("tp") // 2
    rows = own.shape[0]
    for d in range(4):
        at = pl.multiple_of(((y + 4 - d) % 4) * rows, 32)
        out[pl.ds(at, rows), :] = parts[d][...]


def spread_kernel(mine, theirs, out):
    core = lax.axis_index("tp") % 2
    rows = mine.shape[0] // 4
    for y in range(4):
        for side, part in ((core, mine), (1 - core, theirs)):
            at = pl.multiple_of((2 * y + side) * rows, 32)
            out[pl.ds(at, rows), :] = part[y * rows : (y + 1) * rows, :]


def make_collect(parts):
    rows, columns = parts[0].shape
    return pl.pallas_call(
        collect_kernel,
        out_shape=jax.ShapeDtypeStruct((4 * rows, columns), parts[0].dtype),
        in_specs=[vmem_spec()] * 4,
        out_specs=vmem_spec(),
        compiler_params=pltpu.CompilerParams(vmem_limit_bytes=8 * 2**20),
        cost_estimate=lasting(1),
        name="collect",
    )(*parts)


def make_spread(mine, theirs):
    return pl.pallas_call(
        spread_kernel,
        out_shape=jax.ShapeDtypeStruct((2 * mine.shape[0], mine.shape[1]), mine.dtype),
        in_specs=[vmem_spec()] * 2,
        out_specs=vmem_spec(),
        compiler_params=pltpu.CompilerParams(vmem_limit_bytes=12 * 2**20),
        cost_estimate=lasting(1),
        name="spread",
    )(mine, theirs)


def make_messages(flat, tables, theirs, same, other):
    count = len(tables)
    shapes = [
        jax.ShapeDtypeStruct((len(which) * PAIR, COLS), jnp.bfloat16)
        for which in PHASES
        for _ in range(ROUNDS)
    ]
    held, sems = table_scratch(count)
    messages = pl.pallas_call(
        pack_kernel,
        out_shape=tuple(shapes),
        in_specs=[smem_spec()] + [hbm_spec()] * count + [vmem_spec()] * 3,
        out_specs=(vmem_spec(),) * len(shapes),
        scratch_shapes=[
            held,
            pltpu.VMEM((count, 1024, LANES), jnp.float32),
            pltpu.VMEM((count, 1024, LANES), jnp.float32),
            sems,
        ],
        compiler_params=pltpu.CompilerParams(vmem_limit_bytes=VMEM_LIMIT),
        cost_estimate=lasting(1 + 4 * count),
        name="pack",
    )(flat, *tables, theirs, same, other)
    return [messages[n * ROUNDS : (n + 1) * ROUNDS] for n in range(len(PHASES))]


def make_product(acts, parts, first):
    tokens, depth = acts.shape
    tile = tokens // N_TP
    half = N_TP // 2
    return pl.pallas_call(
        product_kernel,
        out_shape=jax.ShapeDtypeStruct((half * tile, COLS), jnp.bfloat16),
        grid_spec=pltpu.PrefetchScalarGridSpec(
            num_scalar_prefetch=1,
            grid=(half,),
            in_specs=[pl.BlockSpec((tile, depth), lambda i, core: (2 * i + core[0], 0))]
            + [pl.BlockSpec((PAIR, COLS), lambda i, core: (0, 0))] * ROUNDS,
            out_specs=pl.BlockSpec((tile, COLS), lambda i, core: (i, 0)),
            scratch_shapes=[pltpu.VMEM((depth, COLS), jnp.bfloat16)],
        ),
        compiler_params=pltpu.CompilerParams(vmem_limit_bytes=16 * 2**20),
        cost_estimate=lasting(3),
        name="product",
    )(first, acts, *parts)


def make_pair(mine, theirs):
    shape = jax.ShapeDtypeStruct((mine.shape[0] // 4, COLS), jnp.bfloat16)
    return pl.pallas_call(
        pair_kernel,
        out_shape=(shape,) * 4,
        in_specs=[vmem_spec()] * 2,
        out_specs=(vmem_spec(),) * 4,
        compiler_params=pltpu.CompilerParams(vmem_limit_bytes=12 * 2**20),
        cost_estimate=lasting(1),
        name="pairsum",
    )(mine, theirs)


def make_update(arrived, where, grad, rounds, begun):
    shape = jax.ShapeDtypeStruct(grad.shape, jnp.float32)
    count = len(rounds)
    operands = [phase[r] for phase in arrived for r in rounds] + [grad] + list(begun)
    aliases = {len(operands) - 3 + k: k for k in range(3)} if begun else {}
    return pl.pallas_call(
        functools.partial(update_kernel, where, rounds, bool(begun)),
        out_shape=(shape,) * 3,
        in_specs=[any_spec()] * len(operands),
        out_specs=(any_spec(),) * 3,
        input_output_aliases=aliases,
        scratch_shapes=[
            pltpu.VMEM((count, 3, PAIR, COLS), jnp.bfloat16),
            pltpu.VMEM((count, PAIR, COLS), jnp.float32),
            pltpu.VMEM((count, 3, PAIR, COLS), jnp.float32),
            pltpu.SemaphoreType.DMA((count, 4)),
            pltpu.SemaphoreType.DMA((count, 3)),
        ],
        compiler_params=pltpu.CompilerParams(vmem_limit_bytes=VMEM_LIMIT),
        cost_estimate=lasting(1 + count),
        name="update",
    )(*operands)


def on_device(old_master, old_momentum, old_variance, flat_offsets, hidden_acts, out_grad):
    siblings = sibling_pairs()
    acts = lax.all_gather(hidden_acts, "fsdp", axis=0, tiled=True)
    tables = [
        jnp.transpose(old, (1, 0, 2)).reshape(TABLE, LANES)
        for old in (old_master, old_momentum, old_variance)
    ]
    tie = lax.optimization_barrier
    swap, edge = make_swap(flat_offsets, tables)
    other = lax.ppermute(edge, AXES, edge_pairs(False))
    same = lax.ppermute(edge, AXES, edge_pairs(True))
    theirs = lax.ppermute(swap, AXES, siblings)
    grad_parts = [lax.ppermute(out_grad, AXES, along_y(d)) for d in range(1, 4)]
    messages = make_messages(flat_offsets, tables, theirs, same, other)
    arrived = [
        [lax.ppermute(lot[r], AXES, round_pairs(r)) for r in range(ROUNDS)] for lot in messages
    ]
    grads_mine = make_collect([out_grad, *grad_parts])
    grads_out = make_spread(grads_mine, lax.ppermute(grads_mine, AXES, siblings))
    where = [None] * 3
    for number, which in enumerate(PHASES):
        for k, tensor in enumerate(which):
            where[tensor] = (number, k * PAIR)
    core = (lax.axis_index("tp") % 2).reshape(1)
    acts, arrived[1][WAIT_FOR] = tie((acts, arrived[1][WAIT_FOR]))
    for_sibling = make_product(acts, arrived[0], 1 - core)
    from_sibling = lax.ppermute(for_sibling, AXES, siblings)
    for_me = make_product(acts, arrived[0], core)
    total, *leaving = make_pair(for_me, from_sibling)
    total = total.astype(jnp.float32)
    for d, part in enumerate(leaving):
        total = total + lax.ppermute(part, AXES, along_y(d + 1)).astype(jnp.float32)
    output = total.astype(jnp.bfloat16)
    weight_grad = lax.dot_general(
        acts, grads_out, (((0,), (0,)), ((), ())), preferred_element_type=jnp.float32
    )
    state = ()
    for rounds in ((0, 1, 2, 3), (4, 5, 6, 7)):
        state = make_update(arrived, where, weight_grad, rounds, state)
    new_master, new_momentum, new_variance = state
    return (output, new_master, new_momentum, new_variance)


def solution(mesh):
    return jax.shard_map(
        on_device,
        mesh=mesh,
        in_specs=(
            P(("fsdp", "tp"), None, None),
            P(("fsdp", "tp"), None, None),
            P(("fsdp", "tp"), None, None),
            P(),
            P("fsdp", "tp"),
            P("tp", "fsdp"),
        ),
        out_specs=(P("tp", "fsdp"), P("tp", "fsdp"), P("tp", "fsdp"), P("tp", "fsdp")),
        check_vma=False,
    )
```

```python
import functools

import jax
import jax.numpy as jnp
from jax import lax
from jax.experimental import pallas as pl
from jax.experimental.pallas import tpu as pltpu
from jax.sharding import PartitionSpec as P

LANES = 128
STEP = 100
AXES = ("fsdp", "tp")
N_FSDP, N_TP = 16, 8
N_ALL = N_FSDP * N_TP
ROW_GRANULES = 64
ROWS = 112
PAIR = 2 * ROWS
SPAN = 128
OWN = ROWS * ROW_GRANULES
COLS = 512
ROUNDS = 8
CHUNK = 16
EDGE = 384
GRAN = 4300
TABLE = 2 * GRAN
FRONT = 2816
BACK = 1400
VMEM_LIMIT = 60 * 2**20

beta_first = 0.9
beta_second = 0.95
epsilon = 1e-08
decay_rate = 0.1
learn_rate = 0.001

WAIT_FOR = 2
PHASES = ((0,), (1, 2))


def source_of(f, t):
    return f * N_TP + t


def target_column(round_id, f, t):
    rv, ru = divmod(round_id, 4)
    x, z, y, c = f // 4, f % 4, t // 2, t % 2
    return ((x + 4 - y + ru + 2 * c) % 4) * 4 + (z + rv + 2 * c) % 4


def sender_block(round_id, f, t):
    rv, ru = divmod(round_id, 4)
    xp, zp, yp, cp = f // 4, f % 4, t // 2, t % 2
    w = (zp + 8 - 2 * cp - rv) % 4
    b, c = w % 2, w // 2
    y = (yp + ru + 2 * c + 4 - xp) % 4
    return b * 4 + y


def all_pairs(target):
    return [
        (source_of(f, t), source_of(*target(f, t))) for f in range(N_FSDP) for t in range(N_TP)
    ]


def round_pairs(round_id):
    return all_pairs(lambda f, t: (target_column(round_id, f, t), f // 2))


def sibling_pairs():
    return all_pairs(lambda f, t: (f, t ^ 1))


def edge_pairs(same_core):
    pairs = []
    for s in range(N_ALL):
        pair, core = s // 2, s % 2
        pair = (pair + (1 if core else -1)) % (N_ALL // 2)
        pairs.append((s, pair * 2 + (core if same_core else 1 - core)))
    return pairs


def along_y(shift):
    return all_pairs(lambda f, t: (f, (t + 2 * shift) % N_TP))


def on_core(body):
    core = lax.axis_index("tp") % 2
    for static in range(2):
        pl.when(core == static)(functools.partial(body, static))


def load_tables(tables, held, sems):
    copies = []
    for k, table in enumerate(tables):
        copy = pltpu.make_async_copy(table, held.at[k, pl.ds(FRONT, TABLE)], sems.at[k])
        copy.start()
        copies.append(copy)
    return copies


def own_rows(held, flat, k, core, row, column):
    s = source_of(lax.axis_index("fsdp"), lax.axis_index("tp"))
    base = (s // 2) * (PAIR * ROW_GRANULES)
    at = (ROWS * core + row) * ROW_GRANULES + column
    stride = 2 * ROW_GRANULES
    cut = flat[2 * s + 1] - base

    def first():
        return held[k, pl.ds(FRONT + 2 * (at + base - flat[2 * s]), 16, stride=stride), :]

    def second():
        return held[k, pl.ds(FRONT + 2 * (at - cut) + 1, 16, stride=stride), :]

    if row < 48:
        return first()
    if row > 48:
        return second()
    ids = lax.broadcasted_iota(jnp.int32, (16, LANES), 0) * ROW_GRANULES
    return jnp.where(ids + at < cut, first(), second())


def swap_kernel(count, flat, *refs):
    tables = refs[:count]
    out, edge, held, sems = refs[count:]
    copies = load_tables(tables, held, sems)
    f, t = lax.axis_index("fsdp"), lax.axis_index("tp")
    s = source_of(f, t)
    left_at = s * OWN - EDGE - flat[2 * s]
    right_at = s * OWN + OWN - flat[2 * s + 1]

    def put(core):
        for k in range(count):
            copies[k].wait()
            at = FRONT + (2 * right_at + 1 if core else 2 * left_at)
            edge[k * EDGE : (k + 1) * EDGE, :] = held[k, pl.ds(at, EDGE, stride=2), :].astype(
                jnp.bfloat16
            )
            for r in range(ROUNDS):
                for q in range(4):
                    column = target_column(r, f, t + 1 - 2 * core) * 4 + q
                    for j in range(SPAN // 16):
                        at = (k * ROUNDS + r) * SPAN + j * 16
                        out[at : at + 16, q * LANES : (q + 1) * LANES] = own_rows(
                            held, flat, k, core, 16 * (j - core), column
                        ).astype(jnp.bfloat16)

    on_core(put)


def pack_kernel(flat, *refs):
    count = 3
    tables = refs[:count]
    theirs, same, other = refs[count : count + 3]
    refs = refs[count + 3 :]
    outs = [refs[n * ROUNDS : (n + 1) * ROUNDS] for n in range(len(PHASES))]
    held, left_edge, right_edge, sems = refs[len(PHASES) * ROUNDS :]
    copies = load_tables(tables, held, sems)
    f, t = lax.axis_index("fsdp"), lax.axis_index("tp")
    s = source_of(f, t)
    base = (s // 2) * (PAIR * ROW_GRANULES)
    low = flat[2 * s - 2 * (t % 2)] - base
    middle = flat[2 * s - 2 * (t % 2) + 2] - base
    high = flat[2 * s - 2 * (t % 2) + 4] - base
    ids = lax.broadcasted_iota(jnp.int32, (16, LANES), 0) * ROW_GRANULES

    def put(core):
        if core == 0:
            from_left, from_right = other, same
        else:
            from_left, from_right = same, other
        for k in range(count):
            at = k * EDGE
            left_edge[k, 0:EDGE, :] = from_left[at : at + EDGE, :].astype(jnp.float32)
            right_edge[k, 1024 - EDGE : 1024, :] = from_right[at : at + EDGE, :].astype(
                jnp.float32
            )
        for k in range(count):
            copies[k].wait()
            phase = [n for n, which in enumerate(PHASES) if k in which][0]
            first_row = PHASES[phase].index(k) * PAIR
            for r in range(ROUNDS):
                out = outs[phase][r]
                for w in range(PAIR // 16):
                    mine = w <= 7 if core == 0 else w >= 6
                    his = w >= 6 if core == 0 else w <= 7
                    j = w - 6 if core == 0 else w
                    at = (k * ROUNDS + r) * SPAN + j * 16
                    row = first_row + w * 16
                    if his and not mine and 0 < w < 13:
                        out[row : row + 16, :] = theirs[at : at + 16, :]
                        continue
                    for q in range(4):
                        column = target_column(r, f, t) * 4 + q
                        lanes = slice(q * LANES, (q + 1) * LANES)
                        place = ids + w * 16 * ROW_GRANULES + column
                        if mine:
                            value = own_rows(held, flat, k, core, 16 * w - ROWS * core, column)
                        if his:
                            other_value = theirs[at : at + 16, lanes].astype(jnp.float32)
                            if mine:
                                own = place < middle if core == 0 else place >= middle
                                value = jnp.where(own, value, other_value)
                            else:
                                value = other_value
                        if w == 0:
                            edge = left_edge[k, pl.ds(column, 16, stride=ROW_GRANULES), :]
                            value = jnp.where(place < low, edge, value)
                        if w == 13:
                            edge = right_edge[k, pl.ds(column, 16, stride=ROW_GRANULES), :]
                            value = jnp.where(place >= high, edge, value)
                        out[row : row + 16, lanes] = value.astype(jnp.bfloat16)

    on_core(put)


def assemble(parts, weight):
    f, t = lax.axis_index("fsdp"), lax.axis_index("tp")
    for r in range(ROUNDS):
        at = pl.multiple_of(sender_block(r, f, t) * PAIR, 32)
        weight[pl.ds(at, PAIR), :] = parts[r][...]


def product_kernel(core, acts, *refs):
    parts, out, weight = refs[:ROUNDS], refs[ROUNDS], refs[ROUNDS + 1]
    pl.when(pl.program_id(0) == 0)(functools.partial(assemble, parts, weight))
    out[...] = jnp.dot(acts[...], weight[...], preferred_element_type=jnp.float32).astype(
        jnp.bfloat16
    )


def pair_kernel(mine, theirs, *outs):
    y = lax.axis_index("tp") // 2
    rows = mine.shape[0] // 4
    for d in range(4):
        at = pl.multiple_of(((y + d) % 4) * rows, 32)
        total = mine[pl.ds(at, rows), :].astype(jnp.float32) + theirs[pl.ds(at, rows), :].astype(
            jnp.float32
        )
        outs[d][...] = total.astype(jnp.bfloat16)


def update_kernel(where, rounds, resumed, *refs):
    n_phase = 1 + max(phase for phase, _ in where)
    count = len(rounds)
    arrived = [refs[p * count : (p + 1) * count] for p in range(n_phase)]
    at = n_phase * count
    grad = refs[at]
    at += 3 if resumed else 0
    new_master, new_momentum, new_variance = refs[at + 1 : at + 4]
    held, grads, results, in_sems, out_sems = refs[at + 4 :]
    f, t = lax.axis_index("fsdp"), lax.axis_index("tp")
    rows = [pl.multiple_of(sender_block(r, f, t) * PAIR, 32) for r in rounds]
    copies = []
    for r in range(count):
        mine = []
        for k in range(3):
            phase, row = where[k]
            mine.append(
                pltpu.make_async_copy(
                    arrived[phase][r].at[pl.ds(row, PAIR)], held.at[r, k], in_sems.at[r, k]
                )
            )
        mine.append(
            pltpu.make_async_copy(grad.at[pl.ds(rows[r], PAIR)], grads.at[r], in_sems.at[r, 3])
        )
        for copy in mine:
            copy.start()
        copies.append(mine)
    scale_first = 1.0 / (1.0 - beta_first**STEP)
    scale_second = 1.0 / (1.0 - beta_second**STEP)
    leaving = []
    for r in range(count):
        for copy in copies[r]:
            copy.wait()

        @pl.loop(0, PAIR // CHUNK, unroll=2)
        def _(step, r=r):
            chunk = pl.ds(pl.multiple_of(step * CHUNK, CHUNK), CHUNK)
            master = held[r, 0, chunk, :].astype(jnp.float32)
            momentum = held[r, 1, chunk, :].astype(jnp.float32)
            variance = held[r, 2, chunk, :].astype(jnp.float32)
            g = grads[r, chunk, :]
            m = beta_first * momentum + (1.0 - beta_first) * g
            v = beta_second * variance + (1.0 - beta_second) * g * g
            scaled = v * scale_second
            below = scaled * lax.rsqrt(scaled) + epsilon
            guess = pl.reciprocal(below, approx=True)
            inverse = guess * (2.0 - below * guess)
            change = (learn_rate * scale_first) * m * inverse
            results[r, 0, chunk, :] = (1.0 - learn_rate * decay_rate) * master - change
            results[r, 1, chunk, :] = m
            results[r, 2, chunk, :] = v

        for k, out in enumerate((new_master, new_momentum, new_variance)):
            copy = pltpu.make_async_copy(
                results.at[r, k], out.at[pl.ds(rows[r], PAIR)], out_sems.at[r, k]
            )
            copy.start()
            leaving.append(copy)
    for copy in leaving:
        copy.wait()


def any_spec():
    return pl.BlockSpec(memory_space=pl.ANY)


def hbm_spec():
    return pl.BlockSpec(memory_space=pltpu.HBM)


def smem_spec():
    return pl.BlockSpec(memory_space=pltpu.SMEM)


def vmem_spec():
    return pl.BlockSpec(memory_space=pltpu.VMEM)


def table_scratch(count):
    return [
        pltpu.VMEM((count, FRONT + TABLE + BACK, LANES), jnp.float32),
        pltpu.SemaphoreType.DMA((count,)),
    ]


def lasting(microseconds):
    return pl.CostEstimate(
        flops=0, bytes_accessed=int(microseconds * 3.3e6), transcendentals=0
    )


def make_swap(flat, tables):
    count = len(tables)
    return pl.pallas_call(
        functools.partial(swap_kernel, count),
        out_shape=(
            jax.ShapeDtypeStruct((count * ROUNDS * SPAN, COLS), jnp.bfloat16),
            jax.ShapeDtypeStruct((count * EDGE, LANES), jnp.bfloat16),
        ),
        in_specs=[smem_spec()] + [hbm_spec()] * count,
        out_specs=(vmem_spec(),) * 2,
        scratch_shapes=table_scratch(count),
        compiler_params=pltpu.CompilerParams(vmem_limit_bytes=VMEM_LIMIT),
        cost_estimate=lasting(1 + 3 * count),
        name="swap",
    )(flat, *tables)


def collect_kernel(own, *refs):
    parts, out = (own, *refs[:3]), refs[3]
    y = lax.axis_index("tp") // 2
    rows = own.shape[0]
    for d in range(4):
        at = pl.multiple_of(((y + 4 - d) % 4) * rows, 32)
        out[pl.ds(at, rows), :] = parts[d][...]


def spread_kernel(mine, theirs, out):
    core = lax.axis_index("tp") % 2
    rows = mine.shape[0] // 4
    for y in range(4):
        for side, part in ((core, mine), (1 - core, theirs)):
            at = pl.multiple_of((2 * y + side) * rows, 32)
            out[pl.ds(at, rows), :] = part[y * rows : (y + 1) * rows, :]


def make_collect(parts):
    rows, columns = parts[0].shape
    return pl.pallas_call(
        collect_kernel,
        out_shape=jax.ShapeDtypeStruct((4 * rows, columns), parts[0].dtype),
        in_specs=[vmem_spec()] * 4,
        out_specs=vmem_spec(),
        compiler_params=pltpu.CompilerParams(vmem_limit_bytes=8 * 2**20),
        cost_estimate=lasting(1),
        name="collect",
    )(*parts)


def make_spread(mine, theirs):
    return pl.pallas_call(
        spread_kernel,
        out_shape=jax.ShapeDtypeStruct((2 * mine.shape[0], mine.shape[1]), mine.dtype),
        in_specs=[vmem_spec()] * 2,
        out_specs=vmem_spec(),
        compiler_params=pltpu.CompilerParams(vmem_limit_bytes=12 * 2**20),
        cost_estimate=lasting(1),
        name="spread",
    )(mine, theirs)


def make_messages(flat, tables, theirs, same, other):
    count = len(tables)
    shapes = [
        jax.ShapeDtypeStruct((len(which) * PAIR, COLS), jnp.bfloat16)
        for which in PHASES
        for _ in range(ROUNDS)
    ]
    held, sems = table_scratch(count)
    messages = pl.pallas_call(
        pack_kernel,
        out_shape=tuple(shapes),
        in_specs=[smem_spec()] + [hbm_spec()] * count + [vmem_spec()] * 3,
        out_specs=(vmem_spec(),) * len(shapes),
        scratch_shapes=[
            held,
            pltpu.VMEM((count, 1024, LANES), jnp.float32),
            pltpu.VMEM((count, 1024, LANES), jnp.float32),
            sems,
        ],
        compiler_params=pltpu.CompilerParams(vmem_limit_bytes=VMEM_LIMIT),
        cost_estimate=lasting(1 + 4 * count),
        name="pack",
    )(flat, *tables, theirs, same, other)
    return [messages[n * ROUNDS : (n + 1) * ROUNDS] for n in range(len(PHASES))]


def make_product(acts, parts, first):
    tokens, depth = acts.shape
    tile = tokens // N_TP
    half = N_TP // 2
    return pl.pallas_call(
        product_kernel,
        out_shape=jax.ShapeDtypeStruct((half * tile, COLS), jnp.bfloat16),
        grid_spec=pltpu.PrefetchScalarGridSpec(
            num_scalar_prefetch=1,
            grid=(half,),
            in_specs=[pl.BlockSpec((tile, depth), lambda i, core: (2 * i + core[0], 0))]
            + [pl.BlockSpec((PAIR, COLS), lambda i, core: (0, 0))] * ROUNDS,
            out_specs=pl.BlockSpec((tile, COLS), lambda i, core: (i, 0)),
            scratch_shapes=[pltpu.VMEM((depth, COLS), jnp.bfloat16)],
        ),
        compiler_params=pltpu.CompilerParams(vmem_limit_bytes=16 * 2**20),
        cost_estimate=lasting(3),
        name="product",
    )(first, acts, *parts)


def make_pair(mine, theirs):
    shape = jax.ShapeDtypeStruct((mine.shape[0] // 4, COLS), jnp.bfloat16)
    return pl.pallas_call(
        pair_kernel,
        out_shape=(shape,) * 4,
        in_specs=[vmem_spec()] * 2,
        out_specs=(vmem_spec(),) * 4,
        compiler_params=pltpu.CompilerParams(vmem_limit_bytes=12 * 2**20),
        cost_estimate=lasting(1),
        name="pairsum",
    )(mine, theirs)


def make_update(arrived, where, grad, rounds, begun):
    shape = jax.ShapeDtypeStruct(grad.shape, jnp.float32)
    count = len(rounds)
    operands = [phase[r] for phase in arrived for r in rounds] + [grad] + list(begun)
    aliases = {len(operands) - 3 + k: k for k in range(3)} if begun else {}
    return pl.pallas_call(
        functools.partial(update_kernel, where, rounds, bool(begun)),
        out_shape=(shape,) * 3,
        in_specs=[any_spec()] * len(operands),
        out_specs=(any_spec(),) * 3,
        input_output_aliases=aliases,
        scratch_shapes=[
            pltpu.VMEM((count, 3, PAIR, COLS), jnp.bfloat16),
            pltpu.VMEM((count, PAIR, COLS), jnp.float32),
            pltpu.VMEM((count, 3, PAIR, COLS), jnp.float32),
            pltpu.SemaphoreType.DMA((count, 4)),
            pltpu.SemaphoreType.DMA((count, 3)),
        ],
        compiler_params=pltpu.CompilerParams(vmem_limit_bytes=VMEM_LIMIT),
        cost_estimate=lasting(1 + count),
        name="update",
    )(*operands)


def on_device(old_master, old_momentum, old_variance, flat_offsets, hidden_acts, out_grad):
    siblings = sibling_pairs()
    acts = lax.all_gather(hidden_acts, "fsdp", axis=0, tiled=True)
    tables = [
        jnp.transpose(old, (1, 0, 2)).reshape(TABLE, LANES)
        for old in (old_master, old_momentum, old_variance)
    ]
    tie = lax.optimization_barrier
    swap, edge = make_swap(flat_offsets, tables)
    other = lax.ppermute(edge, AXES, edge_pairs(False))
    same = lax.ppermute(edge, AXES, edge_pairs(True))
    theirs = lax.ppermute(swap, AXES, siblings)
    grad_parts = [lax.ppermute(out_grad, AXES, along_y(d)) for d in range(1, 4)]
    messages = make_messages(flat_offsets, tables, theirs, same, other)
    first = [lax.ppermute(messages[0][r], AXES, round_pairs(r)) for r in range(ROUNDS)]
    first, second = tie((first, list(messages[1])))
    arrived = [first, [lax.ppermute(second[r], AXES, round_pairs(r)) for r in range(ROUNDS)]]
    grads_mine = make_collect([out_grad, *grad_parts])
    grads_out = make_spread(grads_mine, lax.ppermute(grads_mine, AXES, siblings))
    where = [None] * 3
    for number, which in enumerate(PHASES):
        for k, tensor in enumerate(which):
            where[tensor] = (number, k * PAIR)
    core = (lax.axis_index("tp") % 2).reshape(1)
    acts, arrived[1][:WAIT_FOR] = tie((acts, arrived[1][:WAIT_FOR]))
    for_sibling = make_product(acts, arrived[0], 1 - core)
    from_sibling = lax.ppermute(for_sibling, AXES, siblings)
    for_me = make_product(acts, arrived[0], core)
    total, *leaving = make_pair(for_me, from_sibling)
    total = total.astype(jnp.float32)
    for d, part in enumerate(leaving):
        total = total + lax.ppermute(part, AXES, along_y(d + 1)).astype(jnp.float32)
    output = total.astype(jnp.bfloat16)
    weight_grad = lax.dot_general(
        acts, grads_out, (((0,), (0,)), ((), ())), preferred_element_type=jnp.float32
    )
    state = ()
    for rounds in ((0, 1, 2, 3), (4, 5, 6, 7)):
        state = make_update(arrived, where, weight_grad, rounds, state)
    new_master, new_momentum, new_variance = state
    return (output, new_master, new_momentum, new_variance)


def solution(mesh):
    return jax.shard_map(
        on_device,
        mesh=mesh,
        in_specs=(
            P(("fsdp", "tp"), None, None),
            P(("fsdp", "tp"), None, None),
            P(("fsdp", "tp"), None, None),
            P(),
            P("fsdp", "tp"),
            P("tp", "fsdp"),
        ),
        out_specs=(P("tp", "fsdp"), P("tp", "fsdp"), P("tp", "fsdp"), P("tp", "fsdp")),
        check_vma=False,
    )
```
